32 devices in a mesh: groups: 2 (over y), blk: 4 (over z), dim: 2 (over x), sub: 2 (over core).
Axes of the slice: x: 2, y: 2, z: 4, core: 2. Of those that a mesh axis runs over, the one named last changes fastest.
Arguments:
- queries: bfloat16 [96, 262144], P('blk', ('dim', 'sub')), may hold values from -6 to 6
- train_slab: bfloat16 [1024, 262144], P(('groups', 'blk'), ('dim', 'sub')), parts along dimension 0, may hold values from -6 to 6
- basis_in: bfloat16 [64, 64, 64], P(('dim', 'sub')), may hold values from -0.75 to 0.75
- basis_out: bfloat16 [64, 64, 64], P(('dim', 'sub')), may hold values from -0.75 to 0.75
- eigvals: float32 [64, 64, 64], P(('dim', 'sub')), may hold values from 0.2 to 5
- query_ids: int32 [4, 24], replicated, may hold values from 0 to 23, each once within a row
- example_ids: int32 [8, 128], P(('groups', 'blk')), parts along dimension 0, may hold values from 0 to 127, each once within a row
Outputs:
- scores: float32 [96, 1024], P(('dim', 'sub'), ('groups', 'blk')), parts along dimension 1
The draws below stay inside these ranges and needn't reach their ends.
There are 2 independent parts, one for each index of `groups`. The reference program is written for one: setup_inputs(seed, part) draws one part's arguments, and reference() takes and returns one part's arrays. A program takes and returns all parts, laid end to end along the dimension named above; an argument that names none is the same for every part. Nothing has to cross between parts.
Inputs may be any that keep to these rules, and one draw needn't show every extreme that they name: `query_ids`: each row is a permutation of 0 to 23. `example_ids`: each row is a permutation of 0 to 127.
All inputs are finite; a program needn't handle non-finite values.
Results may differ from the reference program's by a relative error of at most 0.0029.
Values may be sent and summed in bfloat16 or wider, within the bound.
A program may use at most 128 MiB of HBM per device.

```python
import math
import jax
import jax.numpy as jnp
from jax import lax

BLOCKS = 64
PA = 64
PB = 64
EX_DEV = 128
Q_DEV = 24
PROJ = 262144
EXAMPLES = 512
QUERIES = 96
N_BLK = 4


def shard_levels(rng, dims, pieces, low, largest):
    gain, own = 1.0, jax.random.fold_in(rng, 6)
    for axis_at, shards_of in pieces:
        steps = jnp.exp(jax.random.uniform(jax.random.fold_in(own, axis_at), (shards_of,), jnp.float32, low / len(pieces), largest / len(pieces)))
        gain = gain * jnp.repeat(steps, dims[axis_at] // shards_of).reshape([-1 if axis == axis_at else 1 for axis in range(len(dims))])
    return gain


def centred(own_key, extent, deviation, bound, pieces=(), kind=jnp.bfloat16):
    entries = jax.random.normal(own_key, extent, jnp.float32) * deviation
    if len(pieces) > 0:
        entries = shard_levels(own_key, extent, pieces, -0.22, 0.18) * entries
    return jnp.clip(entries, min=-bound, max=bound).astype(kind)


def setup_inputs(seed: int = 0, part: int = 0) -> dict:
    key_of = jax.random.split(jax.random.key(seed), 8)
    part_splits = jax.random.split(jax.random.fold_in(key_of[7], part), 8)
    return {
        "queries": centred(key_of[0], (QUERIES, PROJ), 1.0, 6.0, ((0, 4), (1, 4))),
        "train_slab": centred(part_splits[1], (EXAMPLES, PROJ), 1.0, 6.0, ((0, 4), (1, 4))),
        "basis_in": centred(key_of[2], (BLOCKS, PA, PA), PA ** -0.5, 0.75, ((0, 4),)),
        "basis_out": centred(key_of[3], (BLOCKS, PB, PB), PB ** -0.5, 0.75, ((0, 4),)),
        "eigvals": jnp.clip(jnp.exp(math.log(5.0) - 3.218876 * jax.random.uniform(key_of[4], (BLOCKS, PA, PB), jnp.float32) ** shard_levels(key_of[4], (BLOCKS, PA, PB), ((0, 4),), -0.2, 0.2)), 0.2, 5.0),
        "query_ids": jax.vmap(lambda own: jax.random.permutation(own, Q_DEV))(jax.random.split(key_of[5], N_BLK)).reshape((N_BLK, Q_DEV)).astype(jnp.int32),
        "example_ids": jax.vmap(lambda own: jax.random.permutation(own, EX_DEV))(jax.random.split(part_splits[6], N_BLK)).reshape((N_BLK, EX_DEV)).astype(jnp.int32),
    }


HIGH = lax.Precision.HIGHEST
DAMPING = 0.01


def precondition(blocks, basis_in, basis_out, eigvals):
    left = basis_in.astype(jnp.float32)
    right = basis_out.astype(jnp.float32)
    inner = jnp.einsum('qbac,bad->qbdc', blocks, left, precision=HIGH)
    inner = jnp.einsum('qbdc,bce->qbde', inner, right, precision=HIGH)
    inner = inner / (eigvals + DAMPING)[None]
    outer = jnp.einsum('qbde,bad->qbae', inner, left, precision=HIGH)
    return jnp.einsum('qbae,bce->qbac', outer, right, precision=HIGH)


def reference(queries, train_slab, basis_in, basis_out, eigvals, query_ids, example_ids):
    count = queries.shape[0]
    blocks = queries.astype(jnp.float32).reshape(count, BLOCKS, PA, PB)
    precond = precondition(blocks, basis_in, basis_out, eigvals).reshape(N_BLK, Q_DEV, PROJ)
    query_hot = (query_ids[:, :, None] == jnp.arange(Q_DEV, dtype=jnp.int32)[None, None, :]).astype(jnp.float32)
    ordered = jnp.einsum('jim,jik->jmk', query_hot, precond, precision=HIGH)
    ordered = ordered.reshape(count, PROJ).astype(jnp.bfloat16)
    raw = jnp.dot(ordered, train_slab.T, preferred_element_type=jnp.float32)
    scaled = raw * (1.0 / (PROJ ** 0.5))
    example_hot = (example_ids[:, :, None] == jnp.arange(EX_DEV, dtype=jnp.int32)[None, None, :]).astype(jnp.float32)
    placed = jnp.einsum('qjn,jnm->qjm', scaled.reshape(count, N_BLK, EX_DEV), example_hot, precision=HIGH)
    return placed.reshape(count, N_BLK * EX_DEV)
```

```python
import functools

import jax
import jax.numpy as jnp
from jax import lax
from jax.experimental import pallas as pl
from jax.experimental.pallas import tpu as pltpu
from jax.sharding import PartitionSpec as P

PROJ = 262144
DAMPING = 0.01
MESH = pl.DeviceIdType.MESH
F32 = jnp.float32
BF16 = jnp.bfloat16
SIDE = 64
WIDE = SIDE * SIDE
HALF = WIDE // 2
TILES = WIDE // 128


def parts_of(value):
    high = value.astype(BF16)
    return high, (value - high.astype(F32)).astype(BF16)


def kernel(
    sizes,
    q_hbm, slab_hbm, a_ref, g_ref, eig_ref, qid_ref, eid_ref,
    out_ref,
    q_v, slab, gath, acc, spread, left32, wide, part, landed,
    q_sem, slab_sem, recv_sem, send_sem, red_send, red_recv,
):
    n_grp, n_blk, n_dim, n_sub = sizes
    count = q_hbm.shape[0]
    blocks = a_ref.shape[0]
    per = blocks // n_grp
    n_red = n_dim * n_sub
    y = lax.axis_index("groups")
    z = lax.axis_index("blk")
    dx = lax.axis_index("dim")
    core = lax.axis_index("sub")
    rank = dx * n_sub + core
    has_up = z < n_blk - 1
    has_down = z > 0

    def block_at(plane, t):
        return t * n_grp + plane

    def query_copy(b):
        return pltpu.make_async_copy(
            q_hbm.at[:, pl.ds(pl.multiple_of(b * WIDE, WIDE), WIDE)], q_v.at[b], q_sem.at[b]
        )

    def slab_copy(b):
        cols = pl.ds(pl.multiple_of(b * WIDE, WIDE), WIDE)
        return pltpu.make_async_copy(slab_hbm.at[:, cols], slab.at[:, cols], slab_sem.at[b])

    def order(i):
        turn = i // per
        return block_at(lax.rem(y + turn, n_grp), i - turn * per)

    def start_query(i, carry):
        query_copy(order(i)).start()
        return carry

    def start_slab(i, carry):
        slab_copy(order(i)).start()
        return carry

    lax.fori_loop(0, blocks, start_query, 0)
    lax.fori_loop(0, blocks, start_slab, 0)

    barrier = pltpu.get_barrier_semaphore()

    @pl.when(has_up)
    def _():
        pl.semaphore_signal(barrier, inc=1, device_id={"blk": z + 1}, device_id_type=MESH)

    @pl.when(has_down)
    def _():
        pl.semaphore_signal(barrier, inc=1, device_id={"blk": z - 1}, device_id_type=MESH)

    for step in range(1, n_grp):
        pl.semaphore_signal(
            barrier, inc=1, device_id={"groups": lax.rem(y + step, n_grp)}, device_id_type=MESH
        )

    def peer(step):
        to = lax.rem(rank + step, n_red)
        return to, {"dim": to // n_sub, "sub": lax.rem(to, n_sub)}

    for step in range(1, n_red):
        pl.semaphore_signal(barrier, inc=1, device_id=peer(step)[1], device_id_type=MESH)

    acc[...] = jnp.zeros_like(acc)
    wide[...] = jnp.zeros_like(wide)

    def precondition(b):
        query_copy(b).wait()
        x = q_v[b].astype(F32)
        for i in range(TILES):
            spread[i * count:(i + 1) * count, :] = x[:, i * 128:(i + 1) * 128]
        rows = [spread[pl.ds(q, TILES, stride=count), :] for q in range(count)]
        pairs = count // 2
        lhs = jnp.concatenate(
            [jnp.concatenate([rows[2 * p], rows[2 * p + 1]], axis=1) for p in range(pairs)], axis=0
        ).astype(BF16)
        g = g_ref[b].astype(F32)
        zero = jnp.zeros_like(g)
        low = jnp.concatenate([g, zero], axis=1).astype(BF16)
        high = jnp.concatenate([zero, g], axis=1).astype(BF16)
        wide[0:SIDE, 0:128] = low
        wide[SIDE:2 * SIDE, 128:256] = low
        wide[2 * SIDE:3 * SIDE, 0:128] = high
        wide[3 * SIDE:4 * SIDE, 128:256] = high
        w = wide[...]
        y1 = jnp.dot(lhs, w, preferred_element_type=F32)
        inner = jnp.concatenate(
            [
                jnp.concatenate(
                    [y1[p * TILES:(p + 1) * TILES, 0:128], y1[p * TILES:(p + 1) * TILES, 128:256]],
                    axis=0,
                )
                for p in range(pairs)
            ],
            axis=1,
        )
        left32[...] = a_ref[b].astype(F32)
        left = jnp.concatenate(
            [left32[pl.ds(0, TILES, stride=2), :], left32[pl.ds(1, TILES, stride=2), :]], axis=0
        )
        a_out = left.astype(BF16)
        a_in = left.T.astype(BF16)
        hi, lo = parts_of(inner)
        mid = jnp.dot(a_in, hi, preferred_element_type=F32) + jnp.dot(
            a_in, lo, preferred_element_type=F32
        )
        inv = 1.0 / (eig_ref[b] + DAMPING)
        inv = jnp.concatenate([inv, inv], axis=1)
        mid = jnp.concatenate(
            [mid[:, p * 128:(p + 1) * 128] * inv for p in range(pairs)], axis=1
        )
        hi, lo = parts_of(mid)
        outer = jnp.dot(a_out, hi, preferred_element_type=F32) + jnp.dot(
            a_out, lo, preferred_element_type=F32
        )
        lhs = jnp.concatenate(
            [
                jnp.concatenate(
                    [outer[0:TILES, p * 128:(p + 1) * 128], outer[TILES:, p * 128:(p + 1) * 128]],
                    axis=1,
                )
                for p in range(pairs)
            ],
            axis=0,
        )
        hi, lo = parts_of(lhs)
        nt = (((1,), (1,)), ((), ()))
        res = lax.dot_general(hi, w, nt, preferred_element_type=F32) + lax.dot_general(
            lo, w, nt, preferred_element_type=F32
        )
        for p in range(pairs):
            for k in range(2):
                q = 2 * p + k
                spread[q * TILES:(q + 1) * TILES, :] = res[
                    p * TILES:(p + 1) * TILES, k * 128:(k + 1) * 128
                ]
        cols = [spread[pl.ds(i, count, stride=TILES), :] for i in range(TILES)]
        mine = jnp.concatenate(
            [
                jnp.concatenate(cols[:TILES // 2], axis=1),
                jnp.concatenate(cols[TILES // 2:], axis=1),
            ],
            axis=0,
        )
        gath[z, b] = mine.astype(BF16)

    def dot_in(j, b):
        value = gath[j, b]
        for h in range(2):
            right = slab[:, pl.ds(pl.multiple_of(b * WIDE + h * HALF, HALF), HALF)]
            acc[j, h] += lax.dot_general(
                value, right, (((1,), (1,)), ((), ())), preferred_element_type=F32
            )

    def move(j, b, way):
        if way == 0:
            to = {"blk": z - 1}
        elif way == 1:
            to = {"blk": z + 1}
        else:
            to = {"groups": lax.rem(y + way - 1, n_grp)}
        return pltpu.make_async_remote_copy(
            src_ref=gath.at[j, b],
            dst_ref=gath.at[j, b],
            send_sem=send_sem.at[way, j, b],
            recv_sem=recv_sem.at[j, b],
            device_id=to,
            device_id_type=MESH,
        )

    def across(j, b):
        for step in range(1, n_grp):
            move(j, b, 1 + step).start()

    def along(dist, t):
        b = block_at(y, t)

        @pl.when(z + dist < n_blk)
        def _():
            move(z + dist, b, 0).wait_recv()

            @pl.when(has_down)
            def _():
                move(z + dist, b, 0).start()

            across(z + dist, b)

        @pl.when(z - dist >= 0)
        def _():
            move(z - dist, b, 1).wait_recv()

            @pl.when(has_up)
            def _():
                move(z - dist, b, 1).start()

            across(z - dist, b)

        @pl.when(z + dist < n_blk)
        def _():
            dot_in(z + dist, b)

        @pl.when(z - dist >= 0)
        def _():
            dot_in(z - dist, b)

    def beside(dist, t):
        for step in range(1, n_grp):
            b = block_at(lax.rem(y + step, n_grp), t)

            @pl.when(z + dist < n_blk)
            def _():
                move(z + dist, b, 2).wait_recv()
                dot_in(z + dist, b)

            @pl.when(z - dist >= 0)
            def _():
                move(z - dist, b, 2).wait_recv()
                dot_in(z - dist, b)

    def send_own(b):
        @pl.when(has_down)
        def _():
            move(z, b, 0).start()

        @pl.when(has_up)
        def _():
            move(z, b, 1).start()

    def own(i):
        b = order(i)
        precondition(b)

        @pl.when(i < per)
        def _():
            send_own(b)

        return b

    entry = n_grp - 1 + n_red - 1
    pl.semaphore_wait(barrier, entry + has_up.astype(jnp.int32) + has_down.astype(jnp.int32))

    own_per_step = blocks // per

    def first(t, carry):
        def one(k, inner):
            own(t * own_per_step + k)
            return inner

        lax.fori_loop(0, own_per_step, one, 0)

        @pl.when(t == 0)
        def _():
            def wait_slab(i, inner):
                slab_copy(order(i)).wait()
                return inner

            lax.fori_loop(0, blocks, wait_slab, 0)

        def own_dot(k, inner):
            dot_in(z, order(t * own_per_step + k))
            return inner

        lax.fori_loop(0, own_per_step, own_dot, 0)
        along(1, t)

        @pl.when(t > 0)
        def _():
            beside(1, t - 1)

        return carry

    lax.fori_loop(0, per, first, 0)

    def later(i, carry):
        dist = 2 + i // per
        t = lax.rem(i, per)
        along(dist, t)
        last = i + per - 1
        beside(1 + last // per, lax.rem(last, per))
        return carry

    if n_blk > 2:
        lax.fori_loop(0, per * (n_blk - 2), later, 0)
    beside(n_blk - 1, per - 1)

    for j in range(n_blk):
        part[j] = acc[j, 0, 0:count, :] + acc[j, 1, count:2 * count, :]

    def give(step):
        to, where = peer(step)
        return pltpu.make_async_remote_copy(
            src_ref=part.at[to],
            dst_ref=landed.at[step],
            send_sem=red_send.at[step],
            recv_sem=red_recv.at[step],
            device_id=where,
            device_id_type=MESH,
        )

    for step in range(1, n_red):
        give(step).start()

    examples = slab_hbm.shape[0]
    ids = qid_ref[pl.ds(rank, 1), :]
    q_hot = (
        jnp.broadcast_to(ids, (count, count))
        == lax.broadcasted_iota(jnp.int32, (count, count), 0)
    ).astype(F32)
    e_hot = (
        jnp.broadcast_to(eid_ref[...], (examples, examples))
        == lax.broadcasted_iota(jnp.int32, (examples, examples), 0)
    ).astype(F32)
    total = part[rank]
    for step in range(1, n_red):
        give(step).wait_recv()
        total = total + landed[step]
    total = total * (1.0 / PROJ**0.5)
    total = jnp.dot(q_hot, total, precision=lax.Precision.HIGHEST, preferred_element_type=F32)
    out_ref[...] = lax.dot_general(
        total, e_hot, (((1,), (1,)), ((), ())),
        precision=lax.Precision.HIGHEST, preferred_element_type=F32,
    )
    for step in range(1, n_red):
        give(step).wait_send()

    def drain(i, carry):
        j = i // per
        b = block_at(y, lax.rem(i, per))

        @pl.when((j >= z) & has_down)
        def _():
            move(j, b, 0).wait_send()

        @pl.when((j <= z) & has_up)
        def _():
            move(j, b, 1).wait_send()

        @pl.when(j != z)
        def _():
            for step in range(1, n_grp):
                move(j, b, 1 + step).wait_send()

        return carry

    lax.fori_loop(0, n_blk * per, drain, 0)


def local(sizes, queries, train_slab, basis_in, basis_out, eigvals, query_ids, example_ids):
    n_grp, n_blk, n_dim, n_sub = sizes
    count, width = queries.shape
    examples = train_slab.shape[0]
    blocks = basis_in.shape[0]
    n_red = n_dim * n_sub
    any_spec = pl.BlockSpec(memory_space=pl.ANY)
    vmem = pl.BlockSpec(memory_space=pltpu.VMEM)
    return pl.pallas_call(
        functools.partial(kernel, sizes),
        out_shape=jax.ShapeDtypeStruct((count, examples), F32),
        in_specs=[any_spec, any_spec, vmem, vmem, vmem, vmem, vmem],
        out_specs=vmem,
        scratch_shapes=[
            pltpu.VMEM((blocks, count, WIDE), BF16),
            pltpu.VMEM((examples, width), BF16),
            pltpu.VMEM((n_blk, blocks, 2 * count, HALF), BF16),
            pltpu.VMEM((n_blk, 2, 2 * count, examples), F32),
            pltpu.VMEM((count * TILES, 128), F32),
            pltpu.VMEM((SIDE, SIDE), F32),
            pltpu.VMEM((256, 256), BF16),
            pltpu.VMEM((n_blk, count, examples), F32),
            pltpu.VMEM((n_red, count, examples), F32),
            pltpu.SemaphoreType.DMA((blocks,)),
            pltpu.SemaphoreType.DMA((blocks,)),
            pltpu.SemaphoreType.DMA((n_blk, blocks)),
            pltpu.SemaphoreType.DMA((n_grp + 1, n_blk, blocks)),
            pltpu.SemaphoreType.DMA((n_red,)),
            pltpu.SemaphoreType.DMA((n_red,)),
        ],
        compiler_params=pltpu.CompilerParams(
            collective_id=0, has_side_effects=True, vmem_limit_bytes=50 * 1024 * 1024
        ),
    )(queries, train_slab, basis_in, basis_out, eigvals, query_ids, example_ids)


def solution(mesh):
    sizes = tuple(mesh.shape[name] for name in ("groups", "blk", "dim", "sub"))
    return jax.shard_map(
        functools.partial(local, sizes),
        mesh=mesh,
        in_specs=(
            P("blk", ("dim", "sub")),
            P(("groups", "blk"), ("dim", "sub")),
            P(("dim", "sub"), None, None),
            P(("dim", "sub"), None, None),
            P(("dim", "sub"), None, None),
            P(),
            P(("groups", "blk"), None),
        ),
        out_specs=P(("dim", "sub"), ("groups", "blk")),
        check_vma=False,
    )
```

```python
import functools

import jax
import jax.numpy as jnp
from jax import lax
from jax.experimental import pallas as pl
from jax.experimental.pallas import tpu as pltpu
from jax.sharding import PartitionSpec as P

PROJ = 262144
DAMPING = 0.01
MESH = pl.DeviceIdType.MESH
F32 = jnp.float32
BF16 = jnp.bfloat16
SIDE = 64
WIDE = SIDE * SIDE
HALF = WIDE // 2
TILES = WIDE // 128


def parts_of(value):
    high = value.astype(BF16)
    return high, (value - high.astype(F32)).astype(BF16)


def kernel(
    sizes, plan,
    q_hbm, slab_hbm, a_hbm, g_hbm, eig_hbm, qid_hbm, eid_hbm,
    out_ref,
    q_v, slab, gath, acc, spread, left32, wide, part, landed,
    a_ref, g_ref, eig_ref, qid_ref, eid_ref, ext, accx, partx, landx,
    q_sem, slab_sem, recv_sem, send_sem, red_send, red_recv, in_sem, ext_sem, ret_sem,
):
    n_grp, n_blk, n_dim, n_sub = sizes
    n_off, n_dir = plan
    count = q_hbm.shape[0]
    blocks = a_hbm.shape[0]
    per = blocks // n_grp
    n_red = n_dim * n_sub
    y = lax.axis_index("groups")
    z = lax.axis_index("blk")
    dx = lax.axis_index("dim")
    core = lax.axis_index("sub")
    rank = dx * n_sub + core
    has_up = z < n_blk - 1
    has_down = z > 0
    at_end = (z == 0) | (z == n_blk - 1)

    def off(t):
        return t >= per - n_off

    def straight(t):
        return t >= per - n_dir

    def inside(j):
        return (z > 0) & (z < n_blk - 1) & (j > 0) & (j < n_blk - 1) & (
            (j == z + 1) | (j == z - 1)
        )

    def goes_down(j, t):
        return has_down & (j >= z) & jnp.logical_not((z == 1) & off(t))

    def goes_up(j, t):
        return has_up & (j <= z) & jnp.logical_not((z == n_blk - 2) & off(t))

    def comes(j, t):
        return (j >= 0) & (j < n_blk) & jnp.logical_not(at_end & off(t))

    def crosses(j, t):
        return comes(j, t) & jnp.logical_not(inside(j) & straight(t))

    def block_at(plane, t):
        return t * n_grp + plane

    def query_copy(b):
        return pltpu.make_async_copy(
            q_hbm.at[:, pl.ds(pl.multiple_of(b * WIDE, WIDE), WIDE)], q_v.at[b], q_sem.at[b]
        )

    def slab_copy(b):
        cols = pl.ds(pl.multiple_of(b * WIDE, WIDE), WIDE)
        return pltpu.make_async_copy(slab_hbm.at[:, cols], slab.at[:, cols], slab_sem.at[b])

    def order(i):
        turn = i // per
        t = i - turn * per
        if n_dir:
            t = jnp.where(turn == 0, t, lax.rem(t + per - n_dir, per))
        return block_at(lax.rem(y + turn, n_grp), t)

    def start_query(i, carry):
        query_copy(order(i)).start()
        return carry

    def start_slab(i, carry):
        slab_copy(order(i)).start()
        return carry

    barrier = pltpu.get_barrier_semaphore()

    @pl.when(has_up)
    def _():
        pl.semaphore_signal(barrier, inc=1, device_id={"blk": z + 1}, device_id_type=MESH)

    @pl.when(has_down)
    def _():
        pl.semaphore_signal(barrier, inc=1, device_id={"blk": z - 1}, device_id_type=MESH)

    for step in range(1, n_grp):
        pl.semaphore_signal(
            barrier, inc=1, device_id={"groups": lax.rem(y + step, n_grp)}, device_id_type=MESH
        )

    def peer(step):
        to = lax.rem(rank + step, n_red)
        return to, {"dim": to // n_sub, "sub": lax.rem(to, n_sub)}

    for step in range(1, n_red):
        pl.semaphore_signal(barrier, inc=1, device_id=peer(step)[1], device_id_type=MESH)

    query_copy(order(0)).start()
    small = [
        pltpu.make_async_copy(src, dst, in_sem.at[k])
        for k, (src, dst) in enumerate(
            ((a_hbm, a_ref), (g_hbm, g_ref), (eig_hbm, eig_ref), (qid_hbm, qid_ref), (eid_hbm, eid_ref))
        )
    ]
    for copy in small:
        copy.start()
    lax.fori_loop(1, blocks, start_query, 0)
    lax.fori_loop(0, blocks, start_slab, 0)
    acc[...] = jnp.zeros_like(acc)
    accx[...] = jnp.zeros_like(accx)
    wide[...] = jnp.zeros_like(wide)
    for copy in small:
        copy.wait()

    def precondition(b):
        query_copy(b).wait()
        x = q_v[b].astype(F32)
        for i in range(TILES):
            spread[i * count:(i + 1) * count, :] = x[:, i * 128:(i + 1) * 128]
        rows = [spread[pl.ds(q, TILES, stride=count), :] for q in range(count)]
        pairs = count // 2
        lhs = jnp.concatenate(
            [jnp.concatenate([rows[2 * p], rows[2 * p + 1]], axis=1) for p in range(pairs)], axis=0
        ).astype(BF16)
        g = g_ref[b].astype(F32)
        zero = jnp.zeros_like(g)
        low = jnp.concatenate([g, zero], axis=1).astype(BF16)
        high = jnp.concatenate([zero, g], axis=1).astype(BF16)
        wide[0:SIDE, 0:128] = low
        wide[SIDE:2 * SIDE, 128:256] = low
        wide[2 * SIDE:3 * SIDE, 0:128] = high
        wide[3 * SIDE:4 * SIDE, 128:256] = high
        w = wide[...]
        y1 = jnp.dot(lhs, w, preferred_element_type=F32)
        inner = jnp.concatenate(
            [
                jnp.concatenate(
                    [y1[p * TILES:(p + 1) * TILES, 0:128], y1[p * TILES:(p + 1) * TILES, 128:256]],
                    axis=0,
                )
                for p in range(pairs)
            ],
            axis=1,
        )
        left32[...] = a_ref[b].astype(F32)
        left = jnp.concatenate(
            [left32[pl.ds(0, TILES, stride=2), :], left32[pl.ds(1, TILES, stride=2), :]], axis=0
        )
        a_out = left.astype(BF16)
        a_in = left.T.astype(BF16)
        hi, lo = parts_of(inner)
        mid = jnp.dot(a_in, hi, preferred_element_type=F32) + jnp.dot(
            a_in, lo, preferred_element_type=F32
        )
        inv = 1.0 / (eig_ref[b] + DAMPING)
        inv = jnp.concatenate([inv, inv], axis=1)
        mid = jnp.concatenate(
            [mid[:, p * 128:(p + 1) * 128] * inv for p in range(pairs)], axis=1
        )
        hi, lo = parts_of(mid)
        outer = jnp.dot(a_out, hi, preferred_element_type=F32) + jnp.dot(
            a_out, lo, preferred_element_type=F32
        )
        lhs = jnp.concatenate(
            [
                jnp.concatenate(
                    [outer[0:TILES, p * 128:(p + 1) * 128], outer[TILES:, p * 128:(p + 1) * 128]],
                    axis=1,
                )
                for p in range(pairs)
            ],
            axis=0,
        )
        hi, lo = parts_of(lhs)
        nt = (((1,), (1,)), ((), ()))
        res = lax.dot_general(hi, w, nt, preferred_element_type=F32) + lax.dot_general(
            lo, w, nt, preferred_element_type=F32
        )
        for p in range(pairs):
            for k in range(2):
                q = 2 * p + k
                spread[q * TILES:(q + 1) * TILES, :] = res[
                    p * TILES:(p + 1) * TILES, k * 128:(k + 1) * 128
                ]
        cols = [spread[pl.ds(i, count, stride=TILES), :] for i in range(TILES)]
        mine = jnp.concatenate(
            [
                jnp.concatenate(cols[:TILES // 2], axis=1),
                jnp.concatenate(cols[TILES // 2:], axis=1),
            ],
            axis=0,
        )
        gath[z, b] = mine.astype(BF16)

    def dot_in(j, b):
        value = gath[j, b]
        for h in range(2):
            right = slab[:, pl.ds(pl.multiple_of(b * WIDE + h * HALF, HALF), HALF)]
            acc[j, h] += lax.dot_general(
                value, right, (((1,), (1,)), ((), ())), preferred_element_type=F32
            )

    def dot_for_end(j, k, b):
        value = gath[j, b]
        for h in range(2):
            accx[j, h] += lax.dot_general(
                value, ext[k, :, h * HALF:(h + 1) * HALF], (((1,), (1,)), ((), ())),
                preferred_element_type=F32,
            )

    def move(j, b, way):
        if way == 0:
            to = {"blk": z - 1}
        elif way == 1:
            to = {"blk": z + 1}
        else:
            to = {"groups": lax.rem(y + way - 1, n_grp)}
        return pltpu.make_async_remote_copy(
            src_ref=gath.at[j, b],
            dst_ref=gath.at[j, b],
            send_sem=send_sem.at[way, j, b],
            recv_sem=recv_sem.at[j, b],
            device_id=to,
            device_id_type=MESH,
        )

    def across(j, t):
        @pl.when(crosses(j, t))
        def _():
            for step in range(1, n_grp):
                move(j, block_at(y, t), 1 + step).start()

    def along(dist, t, ready):
        b = block_at(y, t)

        @pl.when(comes(z + dist, t))
        def _():
            move(z + dist, b, 0).wait_recv()

            @pl.when(goes_down(z + dist, t))
            def _():
                move(z + dist, b, 0).start()

            across(z + dist, t)

        @pl.when(comes(z - dist, t))
        def _():
            move(z - dist, b, 1).wait_recv()

            @pl.when(goes_up(z - dist, t))
            def _():
                move(z - dist, b, 1).start()

            across(z - dist, t)

        ready()

        @pl.when(comes(z + dist, t))
        def _():
            dot_in(z + dist, b)

        @pl.when(comes(z - dist, t))
        def _():
            dot_in(z - dist, b)

    def beside(dist, t):
        for step in range(1, n_grp):
            b = block_at(lax.rem(y + step, n_grp), t)

            @pl.when(crosses(z + dist, t))
            def _():
                move(z + dist, b, 2).wait_recv()
                dot_in(z + dist, b)

            @pl.when(crosses(z - dist, t))
            def _():
                move(z - dist, b, 2).wait_recv()
                dot_in(z - dist, b)

    def send_own(i):
        b = order(i)

        @pl.when((i < per) & goes_down(z, i))
        def _():
            move(z, b, 0).start()

        @pl.when((i < per) & goes_up(z, i))
        def _():
            move(z, b, 1).start()

        if n_dir:
            direct = (i >= per) & (i < per + n_dir)

            @pl.when(direct & inside(z - 1))
            def _():
                move(z, b, 0).start()

            @pl.when(direct & inside(z + 1))
            def _():
                move(z, b, 1).start()

    def slab_move(k, plane, t):
        b = block_at(plane, t)
        return pltpu.make_async_remote_copy(
            src_ref=slab_hbm.at[:, pl.ds(pl.multiple_of(b * WIDE, WIDE), WIDE)],
            dst_ref=ext.at[k],
            send_sem=ext_sem.at[0, k],
            recv_sem=ext_sem.at[1, k],
            device_id={"blk": jnp.where(z == 0, 1, n_blk - 2)},
            device_id_type=MESH,
        )

    handed = [(g * n_off + k, g, per - n_off + k) for g in range(n_grp) for k in range(n_off)]

    precondition(order(0))
    entry = n_grp - 1 + n_red - 1
    pl.semaphore_wait(barrier, entry + has_up.astype(jnp.int32) + has_down.astype(jnp.int32))
    send_own(0)

    own_per_step = blocks // per

    def first(t, carry):
        def one(k, inner):
            i = t * own_per_step + k

            @pl.when(i > 0)
            def _():
                precondition(order(i))
                send_own(i)

            return inner

        lax.fori_loop(0, own_per_step, one, 0)

        if n_off:
            @pl.when((t == per // 2) & at_end)
            def _():
                for k, g, u in handed:
                    slab_move(k, g, u).start()

        def ready():
            @pl.when(t == 0)
            def _():
                def wait_slab(i, inner):
                    slab_copy(order(i)).wait()
                    return inner

                lax.fori_loop(0, blocks, wait_slab, 0)

        along(1, t, ready)

        @pl.when(t > 0)
        def _():
            beside(1, t - 1)

        return carry

    lax.fori_loop(0, per, first, 0)

    def nothing():
        return None

    def own_dot(i, carry):
        dot_in(z, order(i))
        return carry

    def later(i, carry):
        dist = 2 + i // per
        t = lax.rem(i, per)
        along(dist, t, nothing)
        last = i + per - 1
        beside(1 + last // per, lax.rem(last, per))

        @pl.when(i < blocks)
        def _():
            own_dot(i, 0)

        return carry

    steps = per * (n_blk - 2)
    if steps:
        lax.fori_loop(0, steps, later, 0)
    if steps < blocks:
        lax.fori_loop(steps, blocks, own_dot, 0)
    beside(n_blk - 1, per - 1)

    def to_end():
        return pltpu.make_async_remote_copy(
            src_ref=partx,
            dst_ref=landx,
            send_sem=ret_sem.at[0],
            recv_sem=ret_sem.at[1],
            device_id={"blk": jnp.where(z == 1, 0, n_blk - 1)},
            device_id_type=MESH,
        )

    if n_dir:
        def direct_in(j):
            @pl.when(inside(j))
            def _():
                for t in range(per - n_dir, per):
                    for step in range(1, n_grp):
                        b = block_at(lax.rem(y + step, n_grp), t)
                        move(j, b, 0).wait_recv()
                        dot_in(j, b)

        direct_in(z + 1)
        direct_in(z - 1)

    if n_off:
        next_to_end = (z == 1) | (z == n_blk - 2)
        end = jnp.where(z == 1, 0, n_blk - 1)

        @pl.when(next_to_end)
        def _():
            for k, g, u in handed:
                slab_move(k, g, u).wait_recv()
                for j in range(n_blk):
                    @pl.when(j != end)
                    def _():
                        dot_for_end(j, k, block_at(g, u))

            for j in range(n_blk):
                partx[j] = accx[j, 0, 0:count, :] + accx[j, 1, count:2 * count, :]
            to_end().start()

    for j in range(n_blk):
        part[j] = acc[j, 0, 0:count, :] + acc[j, 1, count:2 * count, :]

    if n_off:
        @pl.when(at_end)
        def _():
            to_end().wait_recv()
            part[...] += landx[...]

    def give(step):
        to, where = peer(step)
        return pltpu.make_async_remote_copy(
            src_ref=part.at[to],
            dst_ref=landed.at[step],
            send_sem=red_send.at[step],
            recv_sem=red_recv.at[step],
            device_id=where,
            device_id_type=MESH,
        )

    for step in range(1, n_red):
        give(step).start()

    examples = slab_hbm.shape[0]
    ids = qid_ref[pl.ds(rank, 1), :]
    q_hot = (
        jnp.broadcast_to(ids, (count, count))
        == lax.broadcasted_iota(jnp.int32, (count, count), 0)
    ).astype(F32)
    e_hot = (
        jnp.broadcast_to(eid_ref[...], (examples, examples))
        == lax.broadcasted_iota(jnp.int32, (examples, examples), 0)
    ).astype(F32)
    total = part[rank]
    for step in range(1, n_red):
        give(step).wait_recv()
        total = total + landed[step]
    total = total * (1.0 / PROJ**0.5)
    total = jnp.dot(q_hot, total, precision=lax.Precision.HIGHEST, preferred_element_type=F32)
    out_ref[...] = lax.dot_general(
        total, e_hot, (((1,), (1,)), ((), ())),
        precision=lax.Precision.HIGHEST, preferred_element_type=F32,
    )
    for step in range(1, n_red):
        give(step).wait_send()

    def drain(i, carry):
        j = i // per
        t = lax.rem(i, per)
        b = block_at(y, t)

        @pl.when(goes_down(j, t))
        def _():
            move(j, b, 0).wait_send()

        @pl.when(goes_up(j, t))
        def _():
            move(j, b, 1).wait_send()

        @pl.when((j != z) & crosses(j, t))
        def _():
            for step in range(1, n_grp):
                move(j, b, 1 + step).wait_send()

        return carry

    lax.fori_loop(0, n_blk * per, drain, 0)

    if n_dir:
        for t in range(per - n_dir, per):
            b = block_at(lax.rem(y + 1, n_grp), t)

            @pl.when(inside(z - 1))
            def _():
                move(z, b, 0).wait_send()

            @pl.when(inside(z + 1))
            def _():
                move(z, b, 1).wait_send()

    if n_off:
        @pl.when(at_end)
        def _():
            for k, g, u in handed:
                slab_move(k, g, u).wait_send()

        @pl.when(next_to_end)
        def _():
            to_end().wait_send()


def local(sizes, queries, train_slab, basis_in, basis_out, eigvals, query_ids, example_ids):
    n_grp, n_blk, n_dim, n_sub = sizes
    count, width = queries.shape
    examples = train_slab.shape[0]
    blocks = basis_in.shape[0]
    n_red = n_dim * n_sub
    per = blocks // n_grp
    n_off = per // 8 if n_blk >= 4 and n_grp == 2 else 0
    n_dir = per // 2 if n_off else 0
    handed = max(1, n_off * n_grp)
    any_spec = pl.BlockSpec(memory_space=pl.ANY)
    vmem = pl.BlockSpec(memory_space=pltpu.VMEM)
    return pl.pallas_call(
        functools.partial(kernel, sizes, (n_off, n_dir)),
        out_shape=jax.ShapeDtypeStruct((count, examples), F32),
        in_specs=[any_spec] * 7,
        out_specs=vmem,
        scratch_shapes=[
            pltpu.VMEM((blocks, count, WIDE), BF16),
            pltpu.VMEM((examples, width), BF16),
            pltpu.VMEM((n_blk, blocks, 2 * count, HALF), BF16),
            pltpu.VMEM((n_blk, 2, 2 * count, examples), F32),
            pltpu.VMEM((count * TILES, 128), F32),
            pltpu.VMEM((SIDE, SIDE), F32),
            pltpu.VMEM((256, 256), BF16),
            pltpu.VMEM((n_blk, count, examples), F32),
            pltpu.VMEM((n_red, count, examples), F32),
            pltpu.VMEM(basis_in.shape, BF16),
            pltpu.VMEM(basis_out.shape, BF16),
            pltpu.VMEM(eigvals.shape, F32),
            pltpu.VMEM(query_ids.shape, jnp.int32),
            pltpu.VMEM(example_ids.shape, jnp.int32),
            pltpu.VMEM((handed, examples, WIDE), BF16),
            pltpu.VMEM((n_blk, 2, 2 * count, examples), F32),
            pltpu.VMEM((n_blk, count, examples), F32),
            pltpu.VMEM((n_blk, count, examples), F32),
            pltpu.SemaphoreType.DMA((blocks,)),
            pltpu.SemaphoreType.DMA((blocks,)),
            pltpu.SemaphoreType.DMA((n_blk, blocks)),
            pltpu.SemaphoreType.DMA((n_grp + 1, n_blk, blocks)),
            pltpu.SemaphoreType.DMA((n_red,)),
            pltpu.SemaphoreType.DMA((n_red,)),
            pltpu.SemaphoreType.DMA((5,)),
            pltpu.SemaphoreType.DMA((2, handed)),
            pltpu.SemaphoreType.DMA((2,)),
        ],
        compiler_params=pltpu.CompilerParams(
            collective_id=0, has_side_effects=True, vmem_limit_bytes=64 * 1024 * 1024 - 65536
        ),
    )(queries, train_slab, basis_in, basis_out, eigvals, query_ids, example_ids)


def solution(mesh):
    sizes = tuple(mesh.shape[name] for name in ("groups", "blk", "dim", "sub"))
    return jax.shard_map(
        functools.partial(local, sizes),
        mesh=mesh,
        in_specs=(
            P("blk", ("dim", "sub")),
            P(("groups", "blk"), ("dim", "sub")),
            P(("dim", "sub"), None, None),
            P(("dim", "sub"), None, None),
            P(("dim", "sub"), None, None),
            P(),
            P(("groups", "blk"), None),
        ),
        out_specs=P(("dim", "sub"), ("groups", "blk")),
        check_vma=False,
    )
```

```python
import functools

import jax
import jax.numpy as jnp
from jax import lax
from jax.experimental import pallas as pl
from jax.experimental.pallas import tpu as pltpu
from jax.sharding import PartitionSpec as P

PROJ = 262144
DAMPING = 0.01
MESH = pl.DeviceIdType.MESH
F32 = jnp.float32
BF16 = jnp.bfloat16
SIDE = 64
WIDE = SIDE * SIDE
HALF = WIDE // 2
TILES = WIDE // 128


def parts_of(value):
    high = value.astype(BF16)
    return high, (value - high.astype(F32)).astype(BF16)


def kernel(
    sizes, plan,
    q_hbm, slab_hbm, a_hbm, g_hbm, eig_hbm, qid_hbm, eid_hbm,
    out_ref,
    q_v, slab, gath, acc, spread, left32, wide, part, landed,
    a_ref, g_ref, eig_ref, qid_ref, eid_ref, ext, accx, partx, landx,
    q_sem, slab_sem, recv_sem, send_sem, red_send, red_recv, in_sem, ext_sem, ret_sem,
):
    n_grp, n_blk, n_dim, n_sub = sizes
    n_off, n_dir = plan
    count = q_hbm.shape[0]
    blocks = a_hbm.shape[0]
    per = blocks // n_grp
    n_red = n_dim * n_sub
    y = lax.axis_index("groups")
    z = lax.axis_index("blk")
    dx = lax.axis_index("dim")
    core = lax.axis_index("sub")
    rank = dx * n_sub + core
    has_up = z < n_blk - 1
    has_down = z > 0
    at_end = (z == 0) | (z == n_blk - 1)

    def off(t):
        return t >= per - n_off

    def straight(t):
        return t >= per - n_dir

    def inside(j):
        return (z > 0) & (z < n_blk - 1) & (j > 0) & (j < n_blk - 1) & (
            (j == z + 1) | (j == z - 1)
        )

    def goes_down(j, t):
        return has_down & (j >= z) & jnp.logical_not((z == 1) & off(t))

    def goes_up(j, t):
        return has_up & (j <= z) & jnp.logical_not((z == n_blk - 2) & off(t))

    def comes(j, t):
        return (j >= 0) & (j < n_blk) & jnp.logical_not(at_end & off(t))

    def crosses(j, t):
        return comes(j, t) & jnp.logical_not(inside(j) & straight(t))

    def block_at(plane, t):
        return t * n_grp + plane

    def query_copy(b):
        return pltpu.make_async_copy(
            q_hbm.at[:, pl.ds(pl.multiple_of(b * WIDE, WIDE), WIDE)], q_v.at[b], q_sem.at[b]
        )

    def slab_copy(b):
        cols = pl.ds(pl.multiple_of(b * WIDE, WIDE), WIDE)
        return pltpu.make_async_copy(slab_hbm.at[:, cols], slab.at[:, cols], slab_sem.at[b])

    def order(i):
        turn = i // per
        t = i - turn * per
        if n_dir:
            t = jnp.where(turn == 0, t, lax.rem(t + per - n_dir, per))
        return block_at(lax.rem(y + turn, n_grp), t)

    def start_query(i, carry):
        query_copy(order(i)).start()
        return carry

    def start_slab(i, carry):
        slab_copy(order(i)).start()
        return carry

    barrier = pltpu.get_barrier_semaphore()

    @pl.when(has_up)
    def _():
        pl.semaphore_signal(barrier, inc=1, device_id={"blk": z + 1}, device_id_type=MESH)

    @pl.when(has_down)
    def _():
        pl.semaphore_signal(barrier, inc=1, device_id={"blk": z - 1}, device_id_type=MESH)

    for step in range(1, n_grp):
        pl.semaphore_signal(
            barrier, inc=1, device_id={"groups": lax.rem(y + step, n_grp)}, device_id_type=MESH
        )

    def peer(step):
        to = lax.rem(rank + step, n_red)
        return to, {"dim": to // n_sub, "sub": lax.rem(to, n_sub)}

    for step in range(1, n_red):
        pl.semaphore_signal(barrier, inc=1, device_id=peer(step)[1], device_id_type=MESH)

    query_copy(order(0)).start()
    small = [
        pltpu.make_async_copy(src, dst, in_sem.at[k])
        for k, (src, dst) in enumerate(
            ((a_hbm, a_ref), (g_hbm, g_ref), (eig_hbm, eig_ref), (qid_hbm, qid_ref), (eid_hbm, eid_ref))
        )
    ]
    for copy in small:
        copy.start()
    lax.fori_loop(1, blocks, start_query, 0)
    lax.fori_loop(0, blocks, start_slab, 0)
    acc[...] = jnp.zeros_like(acc)
    accx[...] = jnp.zeros_like(accx)
    wide[...] = jnp.zeros_like(wide)
    for copy in small:
        copy.wait()

    def precondition(b):
        query_copy(b).wait()
        x = q_v[b].astype(F32)
        for i in range(TILES):
            spread[i * count:(i + 1) * count, :] = x[:, i * 128:(i + 1) * 128]
        rows = [spread[pl.ds(q, TILES, stride=count), :] for q in range(count)]
        pairs = count // 2
        lhs = jnp.concatenate(
            [jnp.concatenate([rows[2 * p], rows[2 * p + 1]], axis=1) for p in range(pairs)], axis=0
        ).astype(BF16)
        g = g_ref[b].astype(F32)
        zero = jnp.zeros_like(g)
        low = jnp.concatenate([g, zero], axis=1).astype(BF16)
        high = jnp.concatenate([zero, g], axis=1).astype(BF16)
        wide[0:SIDE, 0:128] = low
        wide[SIDE:2 * SIDE, 128:256] = low
        wide[2 * SIDE:3 * SIDE, 0:128] = high
        wide[3 * SIDE:4 * SIDE, 128:256] = high
        w = wide[...]
        y1 = jnp.dot(lhs, w, preferred_element_type=F32)
        inner = jnp.concatenate(
            [
                jnp.concatenate(
                    [y1[p * TILES:(p + 1) * TILES, 0:128], y1[p * TILES:(p + 1) * TILES, 128:256]],
                    axis=0,
                )
                for p in range(pairs)
            ],
            axis=1,
        )
        left32[...] = a_ref[b].astype(F32)
        left = jnp.concatenate(
            [left32[pl.ds(0, TILES, stride=2), :], left32[pl.ds(1, TILES, stride=2), :]], axis=0
        )
        a_out = left.astype(BF16)
        a_in = left.T.astype(BF16)
        hi, lo = parts_of(inner)
        mid = jnp.dot(a_in, hi, preferred_element_type=F32) + jnp.dot(
            a_in, lo, preferred_element_type=F32
        )
        inv = 1.0 / (eig_ref[b] + DAMPING)
        inv = jnp.concatenate([inv, inv], axis=1)
        mid = jnp.concatenate(
            [mid[:, p * 128:(p + 1) * 128] * inv for p in range(pairs)], axis=1
        )
        hi, lo = parts_of(mid)
        outer = jnp.dot(a_out, hi, preferred_element_type=F32) + jnp.dot(
            a_out, lo, preferred_element_type=F32
        )
        lhs = jnp.concatenate(
            [
                jnp.concatenate(
                    [outer[0:TILES, p * 128:(p + 1) * 128], outer[TILES:, p * 128:(p + 1) * 128]],
                    axis=1,
                )
                for p in range(pairs)
            ],
            axis=0,
        )
        hi, lo = parts_of(lhs)
        nt = (((1,), (1,)), ((), ()))
        res = lax.dot_general(hi, w, nt, preferred_element_type=F32) + lax.dot_general(
            lo, w, nt, preferred_element_type=F32
        )
        for p in range(pairs):
            for k in range(2):
                q = 2 * p + k
                spread[q * TILES:(q + 1) * TILES, :] = res[
                    p * TILES:(p + 1) * TILES, k * 128:(k + 1) * 128
                ]
        cols = [spread[pl.ds(i, count, stride=TILES), :] for i in range(TILES)]
        mine = jnp.concatenate(
            [
                jnp.concatenate(cols[:TILES // 2], axis=1),
                jnp.concatenate(cols[TILES // 2:], axis=1),
            ],
            axis=0,
        )
        gath[z, b] = mine.astype(BF16)

    def dot_in(j, b):
        value = gath[j, b]
        for h in range(2):
            right = slab[:, pl.ds(pl.multiple_of(b * WIDE + h * HALF, HALF), HALF)]
            acc[j, h] += lax.dot_general(
                value, right, (((1,), (1,)), ((), ())), preferred_element_type=F32
            )

    def dot_for_end(j, k, b):
        value = gath[j, b]
        for h in range(2):
            accx[j, h] += lax.dot_general(
                value, ext[k, :, h * HALF:(h + 1) * HALF], (((1,), (1,)), ((), ())),
                preferred_element_type=F32,
            )

    def move(j, b, way):
        if way == 0:
            to = {"blk": z - 1}
        elif way == 1:
            to = {"blk": z + 1}
        else:
            to = {"groups": lax.rem(y + way - 1, n_grp)}
        return pltpu.make_async_remote_copy(
            src_ref=gath.at[j, b],
            dst_ref=gath.at[j, b],
            send_sem=send_sem.at[way, j, b],
            recv_sem=recv_sem.at[j, b],
            device_id=to,
            device_id_type=MESH,
        )

    def across(j, t):
        @pl.when(crosses(j, t))
        def _():
            for step in range(1, n_grp):
                move(j, block_at(y, t), 1 + step).start()

    def along(dist, t, ready):
        b = block_at(y, t)

        @pl.when(comes(z + dist, t))
        def _():
            move(z + dist, b, 0).wait_recv()

            @pl.when(goes_down(z + dist, t))
            def _():
                move(z + dist, b, 0).start()

            across(z + dist, t)

        @pl.when(comes(z - dist, t))
        def _():
            move(z - dist, b, 1).wait_recv()

            @pl.when(goes_up(z - dist, t))
            def _():
                move(z - dist, b, 1).start()

            across(z - dist, t)

        ready()

        @pl.when(comes(z + dist, t))
        def _():
            dot_in(z + dist, b)

        @pl.when(comes(z - dist, t))
        def _():
            dot_in(z - dist, b)

    def beside(dist, t):
        for step in range(1, n_grp):
            b = block_at(lax.rem(y + step, n_grp), t)

            @pl.when(crosses(z + dist, t))
            def _():
                move(z + dist, b, 2).wait_recv()
                dot_in(z + dist, b)

            @pl.when(crosses(z - dist, t))
            def _():
                move(z - dist, b, 2).wait_recv()
                dot_in(z - dist, b)

    def send_own(i):
        b = order(i)

        @pl.when((i < per) & goes_down(z, i))
        def _():
            move(z, b, 0).start()

        @pl.when((i < per) & goes_up(z, i))
        def _():
            move(z, b, 1).start()

    def slab_move(k, plane, t):
        b = block_at(plane, t)
        return pltpu.make_async_remote_copy(
            src_ref=slab_hbm.at[:, pl.ds(pl.multiple_of(b * WIDE, WIDE), WIDE)],
            dst_ref=ext.at[k],
            send_sem=ext_sem.at[0, k],
            recv_sem=ext_sem.at[1, k],
            device_id={"blk": jnp.where(z == 0, 1, n_blk - 2)},
            device_id_type=MESH,
        )

    handed = [(g * n_off + k, g, per - n_off + k) for g in range(n_grp) for k in range(n_off)]

    precondition(order(0))
    entry = n_grp - 1 + n_red - 1
    pl.semaphore_wait(barrier, entry + has_up.astype(jnp.int32) + has_down.astype(jnp.int32))
    send_own(0)

    own_per_step = blocks // per

    def first(t, carry):
        def one(k, inner):
            i = t * own_per_step + k

            @pl.when(i > 0)
            def _():
                precondition(order(i))
                send_own(i)

            return inner

        lax.fori_loop(0, own_per_step, one, 0)

        if n_off:
            @pl.when((t == per // 2) & at_end)
            def _():
                for k, g, u in handed:
                    slab_move(k, g, u).start()

        def ready():
            @pl.when(t == 0)
            def _():
                def wait_slab(i, inner):
                    slab_copy(order(i)).wait()
                    return inner

                lax.fori_loop(0, blocks, wait_slab, 0)

        along(1, t, ready)

        @pl.when(t > 0)
        def _():
            beside(1, t - 1)

        return carry

    lax.fori_loop(0, per, first, 0)

    def nothing():
        return None

    def own_dot(i, carry):
        dot_in(z, order(i))
        return carry

    def later(i, carry):
        dist = 2 + i // per
        t = lax.rem(i, per)
        along(dist, t, nothing)
        last = i + per - 1
        beside(1 + last // per, lax.rem(last, per))

        @pl.when(i < blocks)
        def _():
            own_dot(i, 0)

        return carry

    if n_dir:
        for t in range(per - n_dir, per):
            b = block_at(lax.rem(y + 1, n_grp), t)

            @pl.when(inside(z - 1))
            def _():
                move(z, b, 0).start()

            @pl.when(inside(z + 1))
            def _():
                move(z, b, 1).start()

    steps = per * (n_blk - 2)
    if steps:
        lax.fori_loop(0, steps, later, 0)
    if steps < blocks:
        lax.fori_loop(steps, blocks, own_dot, 0)
    beside(n_blk - 1, per - 1)

    def to_end():
        return pltpu.make_async_remote_copy(
            src_ref=partx,
            dst_ref=landx,
            send_sem=ret_sem.at[0],
            recv_sem=ret_sem.at[1],
            device_id={"blk": jnp.where(z == 1, 0, n_blk - 1)},
            device_id_type=MESH,
        )

    if n_dir:
        def direct_in(j):
            @pl.when(inside(j))
            def _():
                for t in range(per - n_dir, per):
                    for step in range(1, n_grp):
                        b = block_at(lax.rem(y + step, n_grp), t)
                        move(j, b, 0).wait_recv()
                        dot_in(j, b)

        direct_in(z + 1)
        direct_in(z - 1)

    if n_off:
        next_to_end = (z == 1) | (z == n_blk - 2)
        end = jnp.where(z == 1, 0, n_blk - 1)

        @pl.when(next_to_end)
        def _():
            for k, g, u in handed:
                slab_move(k, g, u).wait_recv()
                for j in range(n_blk):
                    @pl.when(j != end)
                    def _():
                        dot_for_end(j, k, block_at(g, u))

            for j in range(n_blk):
                partx[j] = accx[j, 0, 0:count, :] + accx[j, 1, count:2 * count, :]
            to_end().start()

    for j in range(n_blk):
        part[j] = acc[j, 0, 0:count, :] + acc[j, 1, count:2 * count, :]

    if n_off:
        @pl.when(at_end)
        def _():
            to_end().wait_recv()
            part[...] += landx[...]

    def give(step):
        to, where = peer(step)
        return pltpu.make_async_remote_copy(
            src_ref=part.at[to],
            dst_ref=landed.at[step],
            send_sem=red_send.at[step],
            recv_sem=red_recv.at[step],
            device_id=where,
            device_id_type=MESH,
        )

    for step in range(1, n_red):
        give(step).start()

    examples = slab_hbm.shape[0]
    ids = qid_ref[pl.ds(rank, 1), :]
    q_hot = (
        jnp.broadcast_to(ids, (count, count))
        == lax.broadcasted_iota(jnp.int32, (count, count), 0)
    ).astype(F32)
    e_hot = (
        jnp.broadcast_to(eid_ref[...], (examples, examples))
        == lax.broadcasted_iota(jnp.int32, (examples, examples), 0)
    ).astype(F32)
    total = part[rank]
    for step in range(1, n_red):
        give(step).wait_recv()
        total = total + landed[step]
    total = total * (1.0 / PROJ**0.5)
    total = jnp.dot(q_hot, total, precision=lax.Precision.HIGHEST, preferred_element_type=F32)
    out_ref[...] = lax.dot_general(
        total, e_hot, (((1,), (1,)), ((), ())),
        precision=lax.Precision.HIGHEST, preferred_element_type=F32,
    )
    for step in range(1, n_red):
        give(step).wait_send()

    def drain(i, carry):
        j = i // per
        t = lax.rem(i, per)
        b = block_at(y, t)

        @pl.when(goes_down(j, t))
        def _():
            move(j, b, 0).wait_send()

        @pl.when(goes_up(j, t))
        def _():
            move(j, b, 1).wait_send()

        @pl.when((j != z) & crosses(j, t))
        def _():
            for step in range(1, n_grp):
                move(j, b, 1 + step).wait_send()

        return carry

    lax.fori_loop(0, n_blk * per, drain, 0)

    if n_dir:
        for t in range(per - n_dir, per):
            b = block_at(lax.rem(y + 1, n_grp), t)

            @pl.when(inside(z - 1))
            def _():
                move(z, b, 0).wait_send()

            @pl.when(inside(z + 1))
            def _():
                move(z, b, 1).wait_send()

    if n_off:
        @pl.when(at_end)
        def _():
            for k, g, u in handed:
                slab_move(k, g, u).wait_send()

        @pl.when(next_to_end)
        def _():
            to_end().wait_send()


def local(sizes, queries, train_slab, basis_in, basis_out, eigvals, query_ids, example_ids):
    n_grp, n_blk, n_dim, n_sub = sizes
    count, width = queries.shape
    examples = train_slab.shape[0]
    blocks = basis_in.shape[0]
    n_red = n_dim * n_sub
    per = blocks // n_grp
    n_off = per // 8 if n_blk >= 4 and n_grp == 2 else 0
    n_dir = per // 2 if n_off else 0
    handed = max(1, n_off * n_grp)
    any_spec = pl.BlockSpec(memory_space=pl.ANY)
    vmem = pl.BlockSpec(memory_space=pltpu.VMEM)
    return pl.pallas_call(
        functools.partial(kernel, sizes, (n_off, n_dir)),
        out_shape=jax.ShapeDtypeStruct((count, examples), F32),
        in_specs=[any_spec] * 7,
        out_specs=vmem,
        scratch_shapes=[
            pltpu.VMEM((blocks, count, WIDE), BF16),
            pltpu.VMEM((examples, width), BF16),
            pltpu.VMEM((n_blk, blocks, 2 * count, HALF), BF16),
            pltpu.VMEM((n_blk, 2, 2 * count, examples), F32),
            pltpu.VMEM((count * TILES, 128), F32),
            pltpu.VMEM((SIDE, SIDE), F32),
            pltpu.VMEM((256, 256), BF16),
            pltpu.VMEM((n_blk, count, examples), F32),
            pltpu.VMEM((n_red, count, examples), F32),
            pltpu.VMEM(basis_in.shape, BF16),
            pltpu.VMEM(basis_out.shape, BF16),
            pltpu.VMEM(eigvals.shape, F32),
            pltpu.VMEM(query_ids.shape, jnp.int32),
            pltpu.VMEM(example_ids.shape, jnp.int32),
            pltpu.VMEM((handed, examples, WIDE), BF16),
            pltpu.VMEM((n_blk, 2, 2 * count, examples), F32),
            pltpu.VMEM((n_blk, count, examples), F32),
            pltpu.VMEM((n_blk, count, examples), F32),
            pltpu.SemaphoreType.DMA((blocks,)),
            pltpu.SemaphoreType.DMA((blocks,)),
            pltpu.SemaphoreType.DMA((n_blk, blocks)),
            pltpu.SemaphoreType.DMA((n_grp + 1, n_blk, blocks)),
            pltpu.SemaphoreType.DMA((n_red,)),
            pltpu.SemaphoreType.DMA((n_red,)),
            pltpu.SemaphoreType.DMA((5,)),
            pltpu.SemaphoreType.DMA((2, handed)),
            pltpu.SemaphoreType.DMA((2,)),
        ],
        compiler_params=pltpu.CompilerParams(
            collective_id=0, has_side_effects=True, vmem_limit_bytes=64 * 1024 * 1024 - 65536
        ),
    )(queries, train_slab, basis_in, basis_out, eigvals, query_ids, example_ids)


def solution(mesh):
    sizes = tuple(mesh.shape[name] for name in ("groups", "blk", "dim", "sub"))
    return jax.shard_map(
        functools.partial(local, sizes),
        mesh=mesh,
        in_specs=(
            P("blk", ("dim", "sub")),
            P(("groups", "blk"), ("dim", "sub")),
            P(("dim", "sub"), None, None),
            P(("dim", "sub"), None, None),
            P(("dim", "sub"), None, None),
            P(),
            P(("groups", "blk"), None),
        ),
        out_specs=P(("dim", "sub"), ("groups", "blk")),
        check_vma=False,
    )
```
